512 devices in a mesh: seqa: 16 (over x, z_lo), seqb: 32 (over y, z_hi, core).
Axes of the slice: x: 4, y: 8, z: 8 (z_hi: 2, z_lo: 4; z = z_hi * 4 + z_lo), core: 2. Of those that a mesh axis runs over, the one named last changes fastest.
Arguments:
- query_rows: bfloat16 [131072, 1024], P(('seqa', 'seqb')), may hold values from -256 to 256
- key_rows: bfloat16 [131072, 1024], P(('seqa', 'seqb')), may hold values from -16 to 16
- value_rows: bfloat16 [131072, 1024], P(('seqa', 'seqb')), may hold values from -16 to 16
Outputs:
- attended: bfloat16 [131072, 1024], P(('seqa', 'seqb'))
The draws below stay inside these ranges and needn't reach their ends.
All inputs are finite; a program needn't handle non-finite values.
Results may differ from the reference program's by a relative error of at most 0.0027.
Values may be sent and summed in bfloat16 or wider, within the bound.
A program may use at most 64 MiB of HBM per device.

```python
import jax
import jax.numpy as jnp
from jax import lax

HEADS = 8
HEAD_DIM = 128
TOK_DEV = 256
HALF_WIN = 256
D = 1024
TOKENS = 131072
RANGE_ONE = 2048
RANGE_TWO = 8192
RANGE_THREE = 32768


def layered_field(key, salt):
    base_key = jax.random.fold_in(key, salt)
    field = jnp.clip(jax.random.normal(jax.random.fold_in(base_key, 0), (TOKENS, D), jnp.float32), -4.0, 4.0)
    for level, factor in enumerate((4, 16, 64, 256)):
        offsets = jnp.clip(jax.random.normal(jax.random.fold_in(base_key, level + 1), (TOKENS // factor, D), jnp.float32), -4.0, 4.0)
        field = field + 0.7 * jnp.repeat(offsets, factor, axis=0)
    return field


def draw_key_rows(key, part):
    field = layered_field(key, 11)
    return field.astype(jnp.bfloat16)


def draw_value_rows(key, part):
    return layered_field(key, 31).astype(jnp.bfloat16)


def draw_query_rows(key, part):
    field = jnp.clip(jax.random.normal(jax.random.fold_in(key, 21), (TOKENS, D), jnp.float32), -4.0, 4.0)
    return field.astype(jnp.bfloat16)


def setup_inputs(seed: int = 0) -> dict:
    seeds = jax.random.split(jax.random.key(seed), 4)
    query_rows = draw_query_rows(jax.random.fold_in(seeds[3], 71), 0)
    key_rows = draw_key_rows(jax.random.fold_in(seeds[3], 71), 0)
    value_rows = draw_value_rows(jax.random.fold_in(seeds[3], 71), 0)
    return dict(query_rows=query_rows, key_rows=key_rows, value_rows=value_rows)


def pooled_means(rows):
    count = rows.shape[0] // 4
    return rows.astype(jnp.float32).reshape(count, 4, rows.shape[1]).mean(axis=1).astype(jnp.bfloat16)


def reference(query_rows, key_rows, value_rows):
    key_one = pooled_means(key_rows)
    key_two = pooled_means(key_one)
    key_three = pooled_means(key_two)
    key_four = pooled_means(key_three)
    value_one = pooled_means(value_rows)
    value_two = pooled_means(value_one)
    value_three = pooled_means(value_two)
    value_four = pooled_means(value_three)
    count_one = RANGE_ONE // 4
    count_two = RANGE_TWO // 16
    count_three = RANGE_THREE // 64
    padded_keys = jnp.pad(key_rows, ((HALF_WIN, HALF_WIN), (0, 0)))
    padded_values = jnp.pad(value_rows, ((HALF_WIN, HALF_WIN), (0, 0)))
    near_count = TOK_DEV + 2 * HALF_WIN
    score_scale = 1.0 / (HEAD_DIM ** 0.5)

    def one_block(block):
        first_row = (block * TOK_DEV).astype(jnp.int32)
        queries = lax.dynamic_slice_in_dim(query_rows, first_row, TOK_DEV, 0)
        near_keys = lax.dynamic_slice_in_dim(padded_keys, first_row, near_count, 0)
        near_values = lax.dynamic_slice_in_dim(padded_values, first_row, near_count, 0)
        start_one = ((first_row // RANGE_ONE) * count_one).astype(jnp.int32)
        start_two = ((first_row // RANGE_TWO) * count_two).astype(jnp.int32)
        start_three = ((first_row // RANGE_THREE) * count_three).astype(jnp.int32)
        keyset = jnp.concatenate([near_keys,
                                  lax.dynamic_slice_in_dim(key_one, start_one, count_one, 0),
                                  lax.dynamic_slice_in_dim(key_two, start_two, count_two, 0),
                                  lax.dynamic_slice_in_dim(key_three, start_three, count_three, 0),
                                  key_four], axis=0)
        valueset = jnp.concatenate([near_values,
                                    lax.dynamic_slice_in_dim(value_one, start_one, count_one, 0),
                                    lax.dynamic_slice_in_dim(value_two, start_two, count_two, 0),
                                    lax.dynamic_slice_in_dim(value_three, start_three, count_three, 0),
                                    value_four], axis=0)
        total_keys = keyset.shape[0]
        query_heads = queries.astype(jnp.float32).reshape(TOK_DEV, HEADS, HEAD_DIM)
        key_heads = keyset.astype(jnp.float32).reshape(total_keys, HEADS, HEAD_DIM)
        value_heads = valueset.astype(jnp.float32).reshape(total_keys, HEADS, HEAD_DIM)
        scores = jnp.einsum("thd,khd->htk", query_heads, key_heads) * score_scale
        column = jnp.arange(near_count, dtype=jnp.int32)[None, :]
        row_index = jnp.arange(TOK_DEV, dtype=jnp.int32)[:, None]
        key_position = first_row - HALF_WIN + column
        near_allowed = (column >= row_index) & (column <= row_index + 2 * HALF_WIN - 1)
        near_allowed = near_allowed & (key_position >= 0) & (key_position < TOKENS)
        far_allowed = jnp.ones((TOK_DEV, total_keys - near_count), dtype=bool)
        allowed = jnp.concatenate([near_allowed, far_allowed], axis=1)[None, :, :]
        masked = jnp.where(allowed, scores, -1e30)
        highest = jnp.max(masked, axis=2, keepdims=True)
        expo = jnp.where(allowed, jnp.exp(masked - highest), 0.0)
        denominator = jnp.sum(expo, axis=2)
        weights = expo.astype(jnp.bfloat16).astype(jnp.float32)
        mixed = jnp.einsum("htk,khd->thd", weights, value_heads)
        mixed = mixed / jnp.transpose(denominator)[:, :, None]
        return mixed.reshape(TOK_DEV, HEADS * HEAD_DIM).astype(jnp.bfloat16)

    blocks = lax.map(one_block, jnp.arange(TOKENS // TOK_DEV, dtype=jnp.int32))
    return blocks.reshape(TOKENS, HEADS * HEAD_DIM)
```

```python
import functools

import jax
import jax.numpy as jnp
from jax import lax
from jax.experimental import pallas as pl
from jax.experimental.pallas import tpu as pltpu
from jax.sharding import PartitionSpec as P

MESH = pl.DeviceIdType.MESH
BF16, F32 = jnp.bfloat16, jnp.float32

HEAD_DIM = 128
BLOCK = 256
NX, NY, NZ, NZ_LO, N_HI = 4, 8, 8, 4, 2
CHIPS = 256
LOCAL_HEADS = 4
COLS = LOCAL_HEADS * HEAD_DIM
EXP2_SCALE = 1.4426950408889634 / HEAD_DIM**0.5
MASKED = -1e30


def pool_matrix(rows, columns):
    row = lax.broadcasted_iota(jnp.int32, (rows, columns), 0)
    column = lax.broadcasted_iota(jnp.int32, (rows, columns), 1)
    return jnp.where((column >> 2) == row, 0.25, 0.0).astype(BF16)


def matmul(a, b):
    return jnp.dot(a, b, preferred_element_type=F32)


def kernel(
    q_hbm, k_hbm, v_hbm, o_hbm,
    near, queries, l1, l2, l3, l4, tile, acc, top, den, result,
    loc_sem, sib_s, sib_r, near_s, near_r, l2z_s, l2z_r, l3z_s, l3z_r, l1_s, l1_r,
    ring2_s, ring2_r, ring3_s, ring3_r, l4_s, l4_r, out_loc, out_s, out_r,
):
    seqa, seqb = lax.axis_index("seqa"), lax.axis_index("seqb")
    x, z_lo = seqa // NZ_LO, seqa % NZ_LO
    y, hi, core = seqb // 4, (seqb // 2) % 2, seqb % 2
    z = hi * NZ_LO + z_lo
    chip = seqa * 16 + seqb // 2

    def at_z(d):
        other = (z + d) % NZ
        return (x * NZ_LO + other % NZ_LO, (y * 2 + other // NZ_LO) * 2 + core)

    def at_y(d):
        return (seqa, (((y + d) % NY) * 2 + hi) * 2 + core)

    def at_x(d):
        return (((x + d) % NX) * NZ_LO + z_lo, seqb)

    def at_chip(c, which):
        return (c // 16, (c % 16) * 2 + which)

    sibling = (seqa, seqb + 1 - 2 * core)
    before, after = (chip + CHIPS - 1) % CHIPS, (chip + 1) % CHIPS
    y_pair = (seqa, ((y + 1 - 2 * (y % 2)) * 2 + hi) * 2 + core)
    y_par = y % 2

    barrier = pltpu.get_barrier_semaphore()
    partners = [sibling, at_chip(before, core), at_chip(after, core)]
    partners += [at_z(d) for d in (1, 2, 3, 5, 6, 7)]
    partners += [at_y(d) for d in (1, 7)] + [at_x(d) for d in (1, 2, 3)]
    for partner in partners:
        pl.semaphore_signal(barrier, inc=1, device_id=partner, device_id_type=MESH)
    pl.semaphore_wait(barrier, len(partners))

    def remote(src, dst, s, r, device):
        return pltpu.make_async_remote_copy(
            src_ref=src, dst_ref=dst, send_sem=s, recv_sem=r, device_id=device, device_id_type=MESH
        )

    mine = pl.ds(pl.multiple_of(core * COLS, COLS), COLS)
    theirs = pl.ds(pl.multiple_of((1 - core) * COLS, COLS), COLS)
    own_rows = pl.ds(pl.multiple_of(core * BLOCK, BLOCK), BLOCK)
    sib_rows = pl.ds(pl.multiple_of((1 - core) * BLOCK, BLOCK), BLOCK)
    own_near = pl.ds(pl.multiple_of(BLOCK + core * BLOCK, BLOCK), BLOCK)
    sib_near = pl.ds(pl.multiple_of(2 * BLOCK - core * BLOCK, BLOCK), BLOCK)

    sib = [
        remote(k_hbm.at[:, theirs], near.at[0, own_near], sib_s.at[0], sib_r.at[0], sibling),
        remote(v_hbm.at[:, theirs], near.at[1, own_near], sib_s.at[1], sib_r.at[1], sibling),
        remote(q_hbm.at[:, theirs], queries.at[own_rows], sib_s.at[2], sib_r.at[2], sibling),
    ]
    loc = [
        pltpu.make_async_copy(k_hbm.at[:, mine], near.at[0, own_near], loc_sem.at[0]),
        pltpu.make_async_copy(v_hbm.at[:, mine], near.at[1, own_near], loc_sem.at[1]),
        pltpu.make_async_copy(q_hbm.at[:, mine], queries.at[own_rows], loc_sem.at[2]),
    ]
    for copy in (sib[0], sib[1], loc[0], loc[1], sib[2], loc[2]):
        copy.start()

    own_to = at_chip(lax.rem(chip + CHIPS - 1 + 2 * core, CHIPS), core)
    sib_to = at_chip(lax.rem(chip + CHIPS + 1 - 2 * core, CHIPS), core)

    def near_copy(second, head, t):
        columns = pl.ds(head * HEAD_DIM, HEAD_DIM)
        if second:
            src = near.at[t, sib_near, columns]
            side, device = core, sib_to
        else:
            src = near.at[t, own_near, columns]
            side, device = 1 - core, own_to
        rows = pl.ds(pl.multiple_of(side * 3 * BLOCK, BLOCK), BLOCK)
        return remote(
            src, near.at[t, rows, columns],
            near_s.at[second, head, t], near_r.at[side, head, t], device,
        )

    loc[0].wait()
    near_first = near_copy(0, 0, 0)
    near_first.start()
    loc[1].wait()
    sib[0].wait_recv()
    sib[1].wait_recv()

    tiles = []
    for t in range(2):
        one = matmul(pool_matrix(128, 512), near[t, BLOCK : 3 * BLOCK, :]).astype(BF16)
        l1[t, y_par, hi] = one
        two = matmul(pool_matrix(32, 128), one).astype(BF16)
        l2[t, y, hi] = two
        tiles.append(matmul(pool_matrix(16, 32), two)[:8])
    tile[z] = jnp.concatenate(tiles, axis=0).astype(BF16)

    l3z = [
        remote(tile.at[z], tile.at[z], l3z_s.at[d], l3z_r.at[d], at_z(d)) for d in range(1, NZ)
    ]
    for copy in l3z:
        copy.start()
    l2z = remote(l2.at[:, y, hi], l2.at[:, y, hi], l2z_s.at[0], l2z_r.at[0], at_z(4))
    l2z.start()
    own_one = l1.at[:, y_par, hi]
    l1y = remote(own_one, own_one, l1_s.at[1], l1_r.at[1], y_pair)
    l1y.start()
    l1z = remote(own_one, own_one, l1_s.at[0], l1_r.at[0], at_z(4))
    l1z.start()
    near_rest = [
        near_copy(second, head, t)
        for head in range(LOCAL_HEADS)
        for second in range(2)
        for t in range(2)
        if (second, head, t) != (0, 0, 0)
    ]

    def attend(head, half, keys, values, allowed, first):
        columns = pl.ds(pl.multiple_of(head * HEAD_DIM, HEAD_DIM), HEAD_DIM)
        q = queries[pl.ds(pl.multiple_of(half * BLOCK, BLOCK), BLOCK), columns]
        scores = lax.dot_general(
            q, keys, (((1,), (1,)), ((), ())), preferred_element_type=F32
        )
        if allowed is not None:
            scores = jnp.where(allowed, scores, MASKED)
        highest = jnp.max(scores, axis=1, keepdims=True)
        slot = head * 2 + half
        if not first:
            old = top[slot]
            highest = jnp.maximum(highest, old)
        weights = jnp.exp2((scores - highest) * EXP2_SCALE)
        total = jnp.sum(weights, axis=1, keepdims=True)
        mixed = matmul(weights.astype(BF16), values)
        if not first:
            shrink = jnp.exp2((old - highest) * EXP2_SCALE)
            total = total + den[slot] * shrink
            mixed = mixed + acc[slot] * shrink
        top[slot] = highest
        den[slot] = total
        acc[slot] = mixed

    def head_columns(head):
        return pl.ds(pl.multiple_of(head * HEAD_DIM, HEAD_DIM), HEAD_DIM)

    loc[2].wait()
    sib[2].wait_recv()

    def inner(i, carry):
        head, half = i // 2, i % 2
        columns = head_columns(head)
        row = lax.broadcasted_iota(jnp.int32, (BLOCK, 2 * BLOCK), 0) + half * BLOCK
        key = lax.broadcasted_iota(jnp.int32, (BLOCK, 2 * BLOCK), 1)
        allowed = (key >= row - BLOCK) & (key <= row + BLOCK - 1)
        attend(
            head, half, near[0, BLOCK : 3 * BLOCK, columns], near[1, BLOCK : 3 * BLOCK, columns],
            allowed, True,
        )
        return carry

    lax.fori_loop(0, 2 * LOCAL_HEADS, inner, 0)

    for copy in l3z:
        copy.wait_recv()
    for t in range(2):
        rows = [tile[i].astype(F32)[8 * t : 8 * t + 8] for i in range(NZ)]
        l3[t, y] = jnp.concatenate(rows, axis=0).astype(BF16)

    l4_copies = []

    def send_four(j, chunk):
        for t in range(2):
            l4[t, x, chunk] = matmul(pool_matrix(16, 64), l3[t, chunk]).astype(BF16)
        part = l4.at[:, x, chunk]
        for d in range(1, NX):
            copy = remote(part, part, l4_s.at[j, d], l4_r.at[j, d], at_x(d))
            copy.start()
            l4_copies.append(copy)

    def ring_step(buf, send, recv, s):
        up, down = (y - (s - 1) + NY) % NY, (y + s - 1) % NY
        if s < 4:
            up, down = buf.at[:, up], buf.at[:, down]
        else:
            up, down = buf.at[0, up], buf.at[1, down]
        copies = [
            remote(up, up, send.at[s - 1, 0], recv.at[s - 1, 0], at_y(1)),
            remote(down, down, send.at[s - 1, 1], recv.at[s - 1, 1], at_y(NY - 1)),
        ]
        for copy in copies:
            copy.start()
        return copies

    ring3 = ring_step(l3, ring3_s, ring3_r, 1)
    send_four(0, y)
    l2z.wait_recv()
    ring2 = ring_step(l2, ring2_s, ring2_r, 1)
    for copy in near_rest:
        copy.start()
    finished = list(ring3) + list(ring2)
    for s in range(1, 5):
        for copy in ring3:
            copy.wait_recv()
        if s < 4:
            ring3 = ring_step(l3, ring3_s, ring3_r, s + 1)
            finished += ring3
            send_four(2 * s - 1, (y - s + NY) % NY)
            send_four(2 * s, (y + s) % NY)
        else:
            send_four(7, (y + 4) % NY)
        for copy in ring2:
            copy.wait_recv()
        if s < 4:
            ring2 = ring_step(l2, ring2_s, ring2_r, s + 1)
            finished += ring2
        if s == 2:
            l1z.wait_recv()
            other_one = l1.at[:, y_par, 1 - hi]
            l1zy = remote(other_one, other_one, l1_s.at[2], l1_r.at[2], y_pair)
            l1zy.start()

    def far(buf):
        def body(i, carry):
            head, half = i // 2, i % 2
            index = (slice(None),) * (len(buf.shape) - 2) + (head_columns(head),)
            keys = buf[(0,) + index].reshape(512, HEAD_DIM)
            values = buf[(1,) + index].reshape(512, HEAD_DIM)
            attend(head, half, keys, values, None, False)
            return carry

        lax.fori_loop(0, 2 * LOCAL_HEADS, body, 0)

    far(l3)
    far(l2)
    l1y.wait_recv()
    l1zy.wait_recv()
    far(l1)
    for copy in l4_copies:
        copy.wait_recv()
    far(l4)

    out = []
    for head in range(LOCAL_HEADS):
        for t in range(2):
            for second in range(2):
                near_copy(second, head, t).wait_recv()
        columns = pl.ds(head * HEAD_DIM, HEAD_DIM)
        for half in range(2):
            edge = pl.ds(half * 3 * BLOCK, BLOCK)
            row = lax.broadcasted_iota(jnp.int32, (BLOCK, BLOCK), 0)
            key = lax.broadcasted_iota(jnp.int32, (BLOCK, BLOCK), 1)
            if half == 0:
                allowed = (key >= row) & (chip > 0)
            else:
                allowed = (key < row) & (chip < CHIPS - 1)
            attend(head, half, near[0, edge, columns], near[1, edge, columns], allowed, False)
            slot = head * 2 + half
            result[half, :, columns] = (acc[slot] / den[slot]).astype(BF16)
        place = pl.ds(pl.multiple_of(core * COLS + head * HEAD_DIM, HEAD_DIM), HEAD_DIM)
        away = remote(
            result.at[1 - core, :, columns], o_hbm.at[:, place],
            out_s.at[head], out_r.at[head], sibling,
        )
        away.start()
        here = pltpu.make_async_copy(
            result.at[core, :, columns], o_hbm.at[:, place], out_loc.at[head]
        )
        here.start()
        out += [(away, here)]
    for copy in sib + l3z + [l2z, l1y, l1z, l1zy] + [near_first] + near_rest + finished + l4_copies:
        copy.wait_send()
    for away, here in out:
        here.wait()
        away.wait()


def local(query_rows, key_rows, value_rows):
    any_space = pl.BlockSpec(memory_space=pl.ANY)
    dma = pltpu.SemaphoreType.DMA
    return pl.pallas_call(
        kernel,
        out_shape=jax.ShapeDtypeStruct(query_rows.shape, query_rows.dtype),
        in_specs=[any_space] * 3,
        out_specs=any_space,
        scratch_shapes=[
            pltpu.VMEM((2, 4 * BLOCK, COLS), BF16),
            pltpu.VMEM((2 * BLOCK, COLS), BF16),
            pltpu.VMEM((2, 2, N_HI, 128, COLS), BF16),
            pltpu.VMEM((2, NY, N_HI, 32, COLS), BF16),
            pltpu.VMEM((2, NY, 64, COLS), BF16),
            pltpu.VMEM((2, NX, NY, 16, COLS), BF16),
            pltpu.VMEM((NZ, 16, COLS), BF16),
            pltpu.VMEM((2 * LOCAL_HEADS, BLOCK, HEAD_DIM), F32),
            pltpu.VMEM((2 * LOCAL_HEADS, BLOCK, 1), F32),
            pltpu.VMEM((2 * LOCAL_HEADS, BLOCK, 1), F32),
            pltpu.VMEM((2, BLOCK, COLS), BF16),
            dma((3,)), dma((3,)), dma((3,)),
            dma((2, LOCAL_HEADS, 2)), dma((2, LOCAL_HEADS, 2)),
            dma((1,)), dma((1,)), dma((NZ,)), dma((NZ,)), dma((3,)), dma((3,)),
            dma((4, 2)), dma((4, 2)), dma((4, 2)), dma((4, 2)),
            dma((NY, NX)), dma((NY, NX)),
            dma((LOCAL_HEADS,)), dma((LOCAL_HEADS,)), dma((LOCAL_HEADS,)),
        ],
        compiler_params=pltpu.CompilerParams(
            collective_id=0, has_side_effects=True, vmem_limit_bytes=48 * 1024 * 1024
        ),
    )(query_rows, key_rows, value_rows)


def solution(mesh):
    spec = P(("seqa", "seqb"), None)
    return jax.shard_map(
        local, mesh=mesh, in_specs=(spec, spec, spec), out_specs=spec, check_vma=False
    )
```

```python
import contextlib

import jax
import jax.numpy as jnp
from jax import lax
from jax.experimental import pallas as pl
from jax.experimental.pallas import tpu as pltpu
from jax.sharding import PartitionSpec as P

MESH = pl.DeviceIdType.MESH
BF16, F32 = jnp.bfloat16, jnp.float32

HEAD_DIM = 128
BLOCK = 256
NX, NY, NZ, NZ_LO, N_HI = 4, 8, 8, 4, 2
CHIPS = 256
LOCAL_HEADS = 4
COLS = LOCAL_HEADS * HEAD_DIM
EXP2_SCALE = 1.4426950408889634 / HEAD_DIM**0.5
MASKED = -1e30
EARLY = 0
WRAP_HEADS = (2, 3)


def scope(name):
    return contextlib.nullcontext()


def arrive(name, *copies):
    with scope(name):
        for copy in copies:
            copy.wait_recv()


def pool_matrix(rows, columns):
    row = lax.broadcasted_iota(jnp.int32, (rows, columns), 0)
    column = lax.broadcasted_iota(jnp.int32, (rows, columns), 1)
    return jnp.where((column >> 2) == row, 0.25, 0.0).astype(BF16)


def matmul(a, b):
    return jnp.dot(a, b, preferred_element_type=F32)


def kernel(
    q_hbm, k_hbm, v_hbm, o_hbm,
    near, queries, l1, l2, l3, l4, tile, acc, top, den, result,
    loc_sem, sib_s, sib_r, near_s, near_r, relay_s, relay_r, wrap_s, one_s, one_r, l2z_s, l2z_r, l3z_s, l3z_r, l1_s, l1_r,
    ring2_s, ring2_r, ring3_s, ring3_r, l4_s, l4_r, out_loc, out_s, out_r,
):
    seqa, seqb = lax.axis_index("seqa"), lax.axis_index("seqb")
    x, z_lo = seqa // NZ_LO, seqa % NZ_LO
    y, hi, core = seqb // 4, (seqb // 2) % 2, seqb % 2
    z = hi * NZ_LO + z_lo
    chip = seqa * 16 + seqb // 2

    def at_z(d):
        other = (z + d) % NZ
        return (x * NZ_LO + other % NZ_LO, (y * 2 + other // NZ_LO) * 2 + core)

    def at_y(d):
        return (seqa, (((y + d) % NY) * 2 + hi) * 2 + core)

    def at_x(d):
        return (((x + d) % NX) * NZ_LO + z_lo, seqb)

    sibling = (seqa, seqb + 1 - 2 * core)
    y_pair = (seqa, ((y + 1 - 2 * (y % 2)) * 2 + hi) * 2 + core)
    y_par = y % 2

    last = ((hi == 0) & (y == NY - 1)) | ((hi == 1) & (y == 0))
    first_of_row = ((hi == 0) & (y == 0)) | ((hi == 1) & (y == NY - 1))
    z_partner = at_z(4)
    rows_of_chips = NX * NZ_LO
    relay_to = (
        jnp.where(last, (seqa + rows_of_chips + 1 - 2 * hi) % rows_of_chips, seqa),
        at_y(NY + 1 - 2 * hi)[1],
    )
    relay_from = (
        jnp.where(first_of_row, (seqa + rows_of_chips + 2 * hi - 1) % rows_of_chips, seqa),
        at_y(NY + 2 * hi - 1)[1],
    )

    wraps = jnp.where(hi == 0, z_lo == NZ_LO - 1, z_lo == 0) & last
    owns_wrap = jnp.where(hi == 1, z_lo == NZ_LO - 1, z_lo == 0) & first_of_row
    takes_wrap = jnp.where(hi == 0, z_lo == 0, z_lo == NZ_LO - 1) & first_of_row
    wrap_to = (
        (seqa + rows_of_chips + 2 * hi - 1) % rows_of_chips,
        (((y + NY + 2 * hi - 1) % NY) * 2 + 1 - hi) * 2 + core,
    )
    wrap_from = wrap_to

    barrier = pltpu.get_barrier_semaphore()
    partners = [sibling, relay_from]
    partners += [at_z(d) for d in range(1, NZ)]
    partners += [at_y(d) for d in (1, 7)] + [at_x(d) for d in (1, 2, 3)]
    with scope("entry"):
        for partner in partners:
            pl.semaphore_signal(barrier, inc=1, device_id=partner, device_id_type=MESH)

        @pl.when(takes_wrap)
        def _():
            pl.semaphore_signal(barrier, inc=1, device_id=wrap_from, device_id_type=MESH)

        pl.semaphore_wait(barrier, len(partners) + jnp.where(owns_wrap, 1, 0))

    def remote(src, dst, s, r, device):
        return pltpu.make_async_remote_copy(
            src_ref=src, dst_ref=dst, send_sem=s, recv_sem=r, device_id=device, device_id_type=MESH
        )

    mine = pl.ds(pl.multiple_of(core * COLS, COLS), COLS)
    theirs = pl.ds(pl.multiple_of((1 - core) * COLS, COLS), COLS)
    own_rows = pl.ds(pl.multiple_of(core * BLOCK, BLOCK), BLOCK)
    sib_rows = pl.ds(pl.multiple_of((1 - core) * BLOCK, BLOCK), BLOCK)
    own_near = pl.ds(pl.multiple_of(BLOCK + core * BLOCK, BLOCK), BLOCK)
    sib_near = pl.ds(pl.multiple_of(2 * BLOCK - core * BLOCK, BLOCK), BLOCK)

    sib = [
        remote(k_hbm.at[:, theirs], near.at[0, own_near], sib_s.at[0], sib_r.at[0], sibling),
        remote(v_hbm.at[:, theirs], near.at[1, own_near], sib_s.at[1], sib_r.at[1], sibling),
        remote(q_hbm.at[:, theirs], queries.at[own_rows], sib_s.at[2], sib_r.at[2], sibling),
    ]
    loc = [
        pltpu.make_async_copy(k_hbm.at[:, mine], near.at[0, own_near], loc_sem.at[0]),
        pltpu.make_async_copy(v_hbm.at[:, mine], near.at[1, own_near], loc_sem.at[1]),
        pltpu.make_async_copy(q_hbm.at[:, mine], queries.at[own_rows], loc_sem.at[2]),
    ]
    for copy in (sib[0], sib[1], loc[0], loc[1], sib[2], loc[2]):
        copy.start()

    own_kind = 1 - (core + hi) % 2

    def near_copy(kind, head, t):
        columns = pl.ds(head * HEAD_DIM, HEAD_DIM)
        block = hi * kind + (1 - hi) * (1 - kind)
        src = near.at[t, pl.ds(pl.multiple_of(BLOCK + block * BLOCK, BLOCK), BLOCK), columns]
        place = 4 * BLOCK * kind + hi * 3 * BLOCK * (1 - kind)
        dst = near.at[t, pl.ds(pl.multiple_of(place, BLOCK), BLOCK), columns]
        return remote(src, dst, near_s.at[kind, head, t], near_r.at[kind, head, t], z_partner)

    loc[0].wait()
    near_first = near_copy(own_kind, 0, 0)
    near_first.start()
    loc[1].wait()
    arrive("sibling rows", sib[0], sib[1])

    tiles = []
    with scope("pooling"):
        for t in range(2):
            one = matmul(pool_matrix(128, 512), near[t, BLOCK : 3 * BLOCK, :]).astype(BF16)
            l1[t, y_par, hi] = one
            two = matmul(pool_matrix(32, 128), one).astype(BF16)
            l2[t, y, hi] = two
            tiles.append(matmul(pool_matrix(16, 32), two)[:8])
        tile[z] = jnp.concatenate(tiles, axis=0).astype(BF16)

    l3z = [
        remote(tile.at[z], tile.at[z], l3z_s.at[d], l3z_r.at[d], at_z(d)) for d in range(1, NZ)
    ]
    for copy in l3z:
        copy.start()
    l2z = remote(l2.at[:, y, hi], l2.at[:, y, hi], l2z_s.at[0], l2z_r.at[0], at_z(4))
    l2z.start()
    own_one = l1.at[:, y_par, hi]
    l1y = remote(own_one, own_one, l1_s.at[1], l1_r.at[1], y_pair)
    l1y.start()
    near_rest = [near_copy(1 - own_kind, 0, 0)] + [
        near_copy(kind, head, t)
        for kind in (1, 0)
        for head in range(LOCAL_HEADS)
        for t in range(2)
        if (head, t) != (0, 0)
    ]
    for copy in near_rest[:EARLY]:
        copy.start()

    def head_columns(head):
        return pl.ds(pl.multiple_of(head * HEAD_DIM, HEAD_DIM), HEAD_DIM)

    def attend(head, first_query, count, keys, values, allowed, first):
        q = queries[first_query : first_query + count, head_columns(head)]
        span = slice(first_query, first_query + count)
        scores = lax.dot_general(keys, q, (((1,), (1,)), ((), ())), preferred_element_type=F32)
        if allowed is not None:
            scores = jnp.where(allowed, scores, MASKED)
        highest = jnp.max(scores, axis=0, keepdims=True)
        if not first:
            old = top[head, :, span]
            highest = jnp.maximum(highest, old)
        weights = jnp.exp2((scores - highest) * EXP2_SCALE)
        total = jnp.sum(weights, axis=0, keepdims=True)
        mixed = lax.dot_general(
            values, weights.astype(BF16), (((0,), (0,)), ((), ())), preferred_element_type=F32
        )
        if not first:
            shrink = jnp.exp2((old - highest) * EXP2_SCALE)
            total = total + den[head, :, span] * shrink
            mixed = mixed + acc[head, :, span] * shrink
        top[head, :, span] = highest
        den[head, :, span] = total
        acc[head, :, span] = mixed

    loc[2].wait()
    sib[2].wait_recv()

    def inner(head, carry):
        columns = head_columns(head)
        key = lax.broadcasted_iota(jnp.int32, (2 * BLOCK, 2 * BLOCK), 0)
        query = lax.broadcasted_iota(jnp.int32, (2 * BLOCK, 2 * BLOCK), 1)
        allowed = (key <= query + BLOCK - 1) & (key >= query - BLOCK)
        keys, values = near[0, BLOCK : 3 * BLOCK, columns], near[1, BLOCK : 3 * BLOCK, columns]
        attend(head, 0, 2 * BLOCK, keys, values, allowed, True)
        return carry

    with scope("inner"):
        lax.fori_loop(0, LOCAL_HEADS, inner, 0, unroll=True)

    arrive("three along z", *l3z)
    arrive("two along z", l2z)
    wrap_copies = [
        remote(
            near.at[:, pl.ds(pl.multiple_of((1 + hi) * BLOCK, BLOCK), BLOCK), columns],
            near.at[:, pl.ds(pl.multiple_of((1 - hi) * 3 * BLOCK, BLOCK), BLOCK), columns],
            wrap_s.at[head], relay_r.at[head], wrap_to,
        )
        for head in WRAP_HEADS
        for columns in [pl.ds(head * HEAD_DIM, HEAD_DIM)]
    ]

    @pl.when(owns_wrap)
    def _():
        for copy in wrap_copies:
            copy.start()

    for copy in near_rest[EARLY:]:
        copy.start()
    for t in range(2):
        rows = [tile[i].astype(F32)[8 * t : 8 * t + 8] for i in range(NZ)]
        l3[t, y] = jnp.concatenate(rows, axis=0).astype(BF16)

    relays, one_parts = [], []

    def partner_one(kind, head):
        columns = pl.ds(head * HEAD_DIM, HEAD_DIM)
        block = (1 - hi) * kind + hi * (1 - kind)
        rows = pl.ds(pl.multiple_of(block * 64, 64), 64)
        place = 4 * BLOCK * kind + (1 - hi) * 3 * BLOCK * (1 - kind)

        for t in range(2):
            block_rows = near[t, pl.ds(pl.multiple_of(place, BLOCK), BLOCK), columns]
            pooled = matmul(pool_matrix(64, BLOCK), block_rows)
            l1[t, y_par, 1 - hi, rows, columns] = pooled.astype(BF16)
        part = l1.at[:, y_par, 1 - hi, rows, columns]
        copy = remote(part, part, one_s.at[kind, head], one_r.at[kind, head], y_pair)
        copy.start()
        one_parts.append(copy)

    def relay(head):
        columns = pl.ds(head * HEAD_DIM, HEAD_DIM)
        arrive("outer %d" % head, near_copy(1, head, 0), near_copy(1, head, 1))
        copy = remote(
            near.at[:, 4 * BLOCK :, columns],
            near.at[:, pl.ds(pl.multiple_of(hi * 3 * BLOCK, BLOCK), BLOCK), columns],
            relay_s.at[head], relay_r.at[head], relay_to,
        )
        relays.append(copy)
        if head in WRAP_HEADS:
            pl.when(jnp.logical_not(wraps))(lambda: copy.start())
        else:
            copy.start()
        partner_one(1, head)

    l4_copies = []

    def send_four(j, chunk):
        for t in range(2):
            l4[t, x, chunk] = matmul(pool_matrix(16, 64), l3[t, chunk]).astype(BF16)
        part = l4.at[:, x, chunk]
        for d in range(1, NX):
            copy = remote(part, part, l4_s.at[j, d], l4_r.at[j, d], at_x(d))
            copy.start()
            l4_copies.append(copy)

    def ring_step(buf, send, recv, s):
        up, down = (y - (s - 1) + NY) % NY, (y + s - 1) % NY
        if s < 4:
            up, down = buf.at[:, up], buf.at[:, down]
        else:
            up, down = buf.at[0, up], buf.at[1, down]
        copies = [
            remote(up, up, send.at[s - 1, 0], recv.at[s - 1, 0], at_y(1)),
            remote(down, down, send.at[s - 1, 1], recv.at[s - 1, 1], at_y(NY - 1)),
        ]
        for copy in copies:
            copy.start()
        return copies

    ring3 = ring_step(l3, ring3_s, ring3_r, 1)
    send_four(0, y)
    ring2 = ring_step(l2, ring2_s, ring2_r, 1)
    finished = list(ring3) + list(ring2)
    for s in range(1, 5):
        arrive("ring3 %d" % s, *ring3)
        if s < 4:
            ring3 = ring_step(l3, ring3_s, ring3_r, s + 1)
            finished += ring3
            send_four(2 * s - 1, (y - s + NY) % NY)
            send_four(2 * s, (y + s) % NY)
        else:
            send_four(7, (y + 4) % NY)
        arrive("ring2 %d" % s, *ring2)
        if s < 4:
            ring2 = ring_step(l2, ring2_s, ring2_r, s + 1)
            finished += ring2
    def far_keys(buf, columns):
        index = (slice(None),) * (len(buf.shape) - 2) + (columns,)
        return [buf[(t,) + index].reshape(512, HEAD_DIM) for t in range(2)]

    def far(buf):
        def body(head, carry):
            attend(head, 0, 2 * BLOCK, *far_keys(buf, head_columns(head)), None, False)
            return carry

        with scope("far"):
            lax.fori_loop(0, LOCAL_HEADS, body, 0, unroll=True)

    for head in range(LOCAL_HEADS):
        relay(head)
    far(l3)
    far(l2)
    arrive("four along x", *l4_copies)
    far(l4)
    arrive("one along y", l1y)

    out = []

    def finish(head):
        columns = pl.ds(head * HEAD_DIM, HEAD_DIM)
        arrive("relay %d" % head, relays[head])
        key = lax.broadcasted_iota(jnp.int32, (BLOCK, BLOCK), 0)
        query = lax.broadcasted_iota(jnp.int32, (BLOCK, BLOCK), 1)
        for half in range(2):
            edge = slice(half * 3 * BLOCK, half * 3 * BLOCK + BLOCK)
            if half == 0:
                allowed = (key >= query) & (chip > 0)
            else:
                allowed = (key < query) & (chip < CHIPS - 1)
            attend(
                head, half * BLOCK, BLOCK, near[0, edge, columns], near[1, edge, columns],
                allowed, False,
            )
        arrive("one %d" % head, one_parts[head], one_parts[LOCAL_HEADS + head])
        attend(head, 0, 2 * BLOCK, *far_keys(l1, columns), None, False)
        mean = (acc[head] / den[head]).T.astype(BF16)
        for half in range(2):
            result[half, :, columns] = mean[half * BLOCK : (half + 1) * BLOCK]
        place = pl.ds(pl.multiple_of(core * COLS + head * HEAD_DIM, HEAD_DIM), HEAD_DIM)
        away = remote(
            result.at[1 - core, :, columns], o_hbm.at[:, place],
            out_s.at[head], out_r.at[head], sibling,
        )
        away.start()
        here = pltpu.make_async_copy(
            result.at[core, :, columns], o_hbm.at[:, place], out_loc.at[head]
        )
        here.start()
        out.append((away, here))

    for head in range(LOCAL_HEADS + 1):
        if head < LOCAL_HEADS:
            arrive("inner %d" % head, near_copy(0, head, 0), near_copy(0, head, 1))
            partner_one(0, head)
        if head > 0:
            finish(head - 1)
    with scope("sent"):
        for copy in sib + l3z + [l2z, l1y, near_first] + near_rest + finished + l4_copies:
            copy.wait_send()
        for copy in one_parts:
            copy.wait_send()
        for head in range(LOCAL_HEADS):
            if head not in WRAP_HEADS:
                relays[head].wait_send()

        @pl.when(jnp.logical_not(wraps))
        def _():
            for head in WRAP_HEADS:
                relays[head].wait_send()

        @pl.when(owns_wrap)
        def _():
            for copy in wrap_copies:
                copy.wait_send()

    with scope("result"):
        for away, here in out:
            here.wait()
            away.wait()


def local(query_rows, key_rows, value_rows):
    any_space = pl.BlockSpec(memory_space=pl.ANY)
    dma = pltpu.SemaphoreType.DMA
    return pl.pallas_call(
        kernel,
        out_shape=jax.ShapeDtypeStruct(query_rows.shape, query_rows.dtype),
        in_specs=[pl.BlockSpec(memory_space=pltpu.HBM)] * 3,
        out_specs=any_space,
        scratch_shapes=[
            pltpu.VMEM((2, 5 * BLOCK, COLS), BF16),
            pltpu.VMEM((2 * BLOCK, COLS), BF16),
            pltpu.VMEM((2, 2, N_HI, 128, COLS), BF16),
            pltpu.VMEM((2, NY, N_HI, 32, COLS), BF16),
            pltpu.VMEM((2, NY, 64, COLS), BF16),
            pltpu.VMEM((2, NX, NY, 16, COLS), BF16),
            pltpu.VMEM((NZ, 16, COLS), BF16),
            pltpu.VMEM((LOCAL_HEADS, HEAD_DIM, 2 * BLOCK), F32),
            pltpu.VMEM((LOCAL_HEADS, 1, 2 * BLOCK), F32),
            pltpu.VMEM((LOCAL_HEADS, 1, 2 * BLOCK), F32),
            pltpu.VMEM((2, BLOCK, COLS), BF16),
            dma((3,)), dma((3,)), dma((3,)),
            dma((2, LOCAL_HEADS, 2)), dma((2, LOCAL_HEADS, 2)),
            dma((LOCAL_HEADS,)), dma((LOCAL_HEADS,)), dma((LOCAL_HEADS,)), dma((2, LOCAL_HEADS)), dma((2, LOCAL_HEADS)),
            dma((1,)), dma((1,)), dma((NZ,)), dma((NZ,)), dma((3,)), dma((3,)),
            dma((4, 2)), dma((4, 2)), dma((4, 2)), dma((4, 2)),
            dma((NY, NX)), dma((NY, NX)),
            dma((LOCAL_HEADS,)), dma((LOCAL_HEADS,)), dma((LOCAL_HEADS,)),
        ],
        compiler_params=pltpu.CompilerParams(
            collective_id=0, has_side_effects=True, vmem_limit_bytes=53 * 1024 * 1024
        ),
    )(query_rows, key_rows, value_rows)


def solution(mesh):
    spec = P(("seqa", "seqb"), None)
    return jax.shard_map(
        local, mesh=mesh, in_specs=(spec, spec, spec), out_specs=spec, check_vma=False
    )
```

```python
import contextlib

import jax
import jax.numpy as jnp
from jax import lax
from jax.experimental import pallas as pl
from jax.experimental.pallas import tpu as pltpu
from jax.sharding import PartitionSpec as P

MESH = pl.DeviceIdType.MESH
BF16, F32 = jnp.bfloat16, jnp.float32

HEAD_DIM = 128
BLOCK = 256
NX, NY, NZ, NZ_LO, N_HI = 4, 8, 8, 4, 2
CHIPS = 256
LOCAL_HEADS = 4
COLS = LOCAL_HEADS * HEAD_DIM
EXP2_SCALE = 1.4426950408889634 / HEAD_DIM**0.5
MASKED = -1e30
EARLY, LATE = 0, 8
WRAP_HEADS = (3,)


def scope(name):
    return contextlib.nullcontext()


def arrive(name, *copies):
    with scope(name):
        for copy in copies:
            copy.wait_recv()


def pool_matrix(rows, columns):
    row = lax.broadcasted_iota(jnp.int32, (rows, columns), 0)
    column = lax.broadcasted_iota(jnp.int32, (rows, columns), 1)
    return jnp.where((column >> 2) == row, 0.25, 0.0).astype(BF16)


def matmul(a, b):
    return jnp.dot(a, b, preferred_element_type=F32)


def kernel(
    q_hbm, k_hbm, v_hbm, o_hbm,
    near, queries, l1, l2, l3, l4, tile, acc, top, den, result,
    loc_sem, sib_s, sib_r, near_s, near_r, relay_s, relay_r, wrap_s, shift_s, shift_r, onward_s, one_s, one_r, l2z_s, l2z_r, l3z_s, l3z_r, l1_s, l1_r,
    ring2_s, ring2_r, ring3_s, ring3_r, l4_s, l4_r, out_loc, out_s, out_r,
):
    seqa, seqb = lax.axis_index("seqa"), lax.axis_index("seqb")
    x, z_lo = seqa // NZ_LO, seqa % NZ_LO
    y, hi, core = seqb // 4, (seqb // 2) % 2, seqb % 2
    z = hi * NZ_LO + z_lo
    chip = seqa * 16 + seqb // 2

    def at_z(d):
        other = (z + d) % NZ
        return (x * NZ_LO + other % NZ_LO, (y * 2 + other // NZ_LO) * 2 + core)

    def at_y(d):
        return (seqa, (((y + d) % NY) * 2 + hi) * 2 + core)

    def at_x(d):
        return (((x + d) % NX) * NZ_LO + z_lo, seqb)

    sibling = (seqa, seqb + 1 - 2 * core)
    y_pair = (seqa, ((y + 1 - 2 * (y % 2)) * 2 + hi) * 2 + core)
    y_par = y % 2

    last = ((hi == 0) & (y == NY - 1)) | ((hi == 1) & (y == 0))
    first_of_row = ((hi == 0) & (y == 0)) | ((hi == 1) & (y == NY - 1))
    z_partner = at_z(4)
    rows_of_chips = NX * NZ_LO
    relay_to = (
        jnp.where(last, (seqa + rows_of_chips + 1 - 2 * hi) % rows_of_chips, seqa),
        at_y(NY + 1 - 2 * hi)[1],
    )
    relay_from = (
        jnp.where(first_of_row, (seqa + rows_of_chips + 2 * hi - 1) % rows_of_chips, seqa),
        at_y(NY + 2 * hi - 1)[1],
    )

    wraps = jnp.where(hi == 0, z_lo == NZ_LO - 1, z_lo == 0) & last
    owns_wrap = jnp.where(hi == 1, z_lo == NZ_LO - 1, z_lo == 0) & first_of_row
    takes_wrap = jnp.where(hi == 0, z_lo == 0, z_lo == NZ_LO - 1) & first_of_row
    shifted = jnp.where(hi == 0, z_lo > 0, z_lo < NZ_LO - 1) & last
    wrap_to = (
        (seqa + rows_of_chips + 2 * hi - 1) % rows_of_chips,
        (((y + NY + 2 * hi - 1) % NY) * 2 + 1 - hi) * 2 + core,
    )
    wrap_from = wrap_to

    barrier = pltpu.get_barrier_semaphore()
    partners = [sibling, relay_from]
    partners += [at_z(d) for d in range(1, NZ)]
    partners += [at_y(d) for d in (1, 7)] + [at_x(d) for d in (1, 2, 3)]
    with scope("entry"):
        for partner in partners:
            pl.semaphore_signal(barrier, inc=1, device_id=partner, device_id_type=MESH)

        @pl.when(takes_wrap)
        def _():
            pl.semaphore_signal(barrier, inc=1, device_id=wrap_from, device_id_type=MESH)

        pl.semaphore_wait(barrier, len(partners) + jnp.where(owns_wrap, 1, 0))

    def remote(src, dst, s, r, device):
        return pltpu.make_async_remote_copy(
            src_ref=src, dst_ref=dst, send_sem=s, recv_sem=r, device_id=device, device_id_type=MESH
        )

    mine = pl.ds(pl.multiple_of(core * COLS, COLS), COLS)
    theirs = pl.ds(pl.multiple_of((1 - core) * COLS, COLS), COLS)
    own_rows = pl.ds(pl.multiple_of(core * BLOCK, BLOCK), BLOCK)
    sib_rows = pl.ds(pl.multiple_of((1 - core) * BLOCK, BLOCK), BLOCK)
    own_near = pl.ds(pl.multiple_of(BLOCK + core * BLOCK, BLOCK), BLOCK)
    sib_near = pl.ds(pl.multiple_of(2 * BLOCK - core * BLOCK, BLOCK), BLOCK)

    sib = [
        remote(k_hbm.at[:, theirs], near.at[0, own_near], sib_s.at[0], sib_r.at[0], sibling),
        remote(v_hbm.at[:, theirs], near.at[1, own_near], sib_s.at[1], sib_r.at[1], sibling),
        remote(q_hbm.at[:, theirs], queries.at[own_rows], sib_s.at[2], sib_r.at[2], sibling),
    ]
    loc = [
        pltpu.make_async_copy(k_hbm.at[:, mine], near.at[0, own_near], loc_sem.at[0]),
        pltpu.make_async_copy(v_hbm.at[:, mine], near.at[1, own_near], loc_sem.at[1]),
        pltpu.make_async_copy(q_hbm.at[:, mine], queries.at[own_rows], loc_sem.at[2]),
    ]
    for copy in (sib[0], sib[1], loc[0], loc[1], sib[2], loc[2]):
        copy.start()

    own_kind = 1 - (core + hi) % 2

    def near_copy(kind, head, t):
        columns = pl.ds(head * HEAD_DIM, HEAD_DIM)
        block = hi * kind + (1 - hi) * (1 - kind)
        src = near.at[t, pl.ds(pl.multiple_of(BLOCK + block * BLOCK, BLOCK), BLOCK), columns]
        place = 4 * BLOCK * kind + hi * 3 * BLOCK * (1 - kind)
        dst = near.at[t, pl.ds(pl.multiple_of(place, BLOCK), BLOCK), columns]
        return remote(src, dst, near_s.at[kind, head, t], near_r.at[kind, head, t], z_partner)

    loc[0].wait()
    near_first = near_copy(own_kind, 0, 0)
    near_first.start()
    loc[1].wait()
    arrive("sibling rows", sib[0], sib[1])

    tiles = []
    with scope("pooling"):
        for t in range(2):
            one = matmul(pool_matrix(128, 512), near[t, BLOCK : 3 * BLOCK, :]).astype(BF16)
            l1[t, y_par, hi] = one
            two = matmul(pool_matrix(32, 128), one).astype(BF16)
            l2[t, y, hi] = two
            tiles.append(matmul(pool_matrix(16, 32), two)[:8])
        tile[z] = jnp.concatenate(tiles, axis=0).astype(BF16)

    l3z = [
        remote(tile.at[z], tile.at[z], l3z_s.at[d], l3z_r.at[d], at_z(d)) for d in range(1, NZ)
    ]
    for copy in l3z:
        copy.start()
    l2z = remote(l2.at[:, y, hi], l2.at[:, y, hi], l2z_s.at[0], l2z_r.at[0], at_z(4))
    l2z.start()
    own_one = l1.at[:, y_par, hi]
    l1y = remote(own_one, own_one, l1_s.at[1], l1_r.at[1], y_pair)
    l1y.start()
    near_rest = [near_copy(1 - own_kind, 0, 0)] + [
        near_copy(kind, head, t)
        for kind in (1, 0)
        for head in range(LOCAL_HEADS)
        for t in range(2)
        if (head, t) != (0, 0)
    ]
    for copy in near_rest[:EARLY]:
        copy.start()

    def head_columns(head):
        return pl.ds(pl.multiple_of(head * HEAD_DIM, HEAD_DIM), HEAD_DIM)

    def attend(head, first_query, count, keys, values, allowed, first):
        q = queries[first_query : first_query + count, head_columns(head)]
        span = slice(first_query, first_query + count)
        scores = lax.dot_general(keys, q, (((1,), (1,)), ((), ())), preferred_element_type=F32)
        if allowed is not None:
            scores = jnp.where(allowed, scores, MASKED)
        highest = jnp.max(scores, axis=0, keepdims=True)
        if not first:
            old = top[head, :, span]
            highest = jnp.maximum(highest, old)
        weights = jnp.exp2((scores - highest) * EXP2_SCALE)
        total = jnp.sum(weights, axis=0, keepdims=True)
        mixed = lax.dot_general(
            values, weights.astype(BF16), (((0,), (0,)), ((), ())), preferred_element_type=F32
        )
        if not first:
            shrink = jnp.exp2((old - highest) * EXP2_SCALE)
            total = total + den[head, :, span] * shrink
            mixed = mixed + acc[head, :, span] * shrink
        top[head, :, span] = highest
        den[head, :, span] = total
        acc[head, :, span] = mixed

    loc[2].wait()
    sib[2].wait_recv()

    def inner(head, carry):
        columns = head_columns(head)
        key = lax.broadcasted_iota(jnp.int32, (2 * BLOCK, 2 * BLOCK), 0)
        query = lax.broadcasted_iota(jnp.int32, (2 * BLOCK, 2 * BLOCK), 1)
        allowed = (key <= query + BLOCK - 1) & (key >= query - BLOCK)
        keys, values = near[0, BLOCK : 3 * BLOCK, columns], near[1, BLOCK : 3 * BLOCK, columns]
        attend(head, 0, 2 * BLOCK, keys, values, allowed, True)
        return carry

    with scope("inner"):
        lax.fori_loop(0, LOCAL_HEADS, inner, 0, unroll=True)

    arrive("three along z", *l3z)
    arrive("two along z", l2z)
    wrap_copies = [
        remote(
            near.at[:, pl.ds(pl.multiple_of((1 + hi) * BLOCK, BLOCK), BLOCK), columns],
            near.at[:, pl.ds(pl.multiple_of((1 - hi) * 3 * BLOCK, BLOCK), BLOCK), columns],
            wrap_s.at[head], relay_r.at[head], wrap_to,
        )
        for head in WRAP_HEADS
        for columns in [pl.ds(head * HEAD_DIM, HEAD_DIM)]
    ]

    @pl.when(owns_wrap)
    def _():
        for copy in wrap_copies:
            copy.start()

    for copy in near_rest[EARLY:LATE]:
        copy.start()
    for t in range(2):
        rows = [tile[i].astype(F32)[8 * t : 8 * t + 8] for i in range(NZ)]
        l3[t, y] = jnp.concatenate(rows, axis=0).astype(BF16)

    relays, one_parts = [], []

    def partner_one(kind, head):
        columns = pl.ds(head * HEAD_DIM, HEAD_DIM)
        block = (1 - hi) * kind + hi * (1 - kind)
        rows = pl.ds(pl.multiple_of(block * 64, 64), 64)
        place = 4 * BLOCK * kind + (1 - hi) * 3 * BLOCK * (1 - kind)

        for t in range(2):
            block_rows = near[t, pl.ds(pl.multiple_of(place, BLOCK), BLOCK), columns]
            pooled = matmul(pool_matrix(64, BLOCK), block_rows)
            l1[t, y_par, 1 - hi, rows, columns] = pooled.astype(BF16)
        part = l1.at[:, y_par, 1 - hi, rows, columns]
        copy = remote(part, part, one_s.at[kind, head], one_r.at[kind, head], y_pair)
        copy.start()
        one_parts.append(copy)

    def shift_copy(head):
        columns = pl.ds(head * HEAD_DIM, HEAD_DIM)
        return remote(
            near.at[:, 4 * BLOCK : 5 * BLOCK, columns], near.at[:, 5 * BLOCK :, columns],
            shift_s.at[head], shift_r.at[head], at_z(NZ + 1 - 2 * hi),
        )

    def onward_copy(head):
        columns = pl.ds(head * HEAD_DIM, HEAD_DIM)
        return remote(
            near.at[:, 5 * BLOCK :, columns],
            near.at[:, pl.ds(pl.multiple_of(hi * 3 * BLOCK, BLOCK), BLOCK), columns],
            onward_s.at[head], relay_r.at[head], at_y(NY + 1 - 2 * hi),
        )

    def relay(head):
        columns = pl.ds(head * HEAD_DIM, HEAD_DIM)
        arrive("outer %d" % head, near_copy(1, head, 0), near_copy(1, head, 1))
        copy = remote(
            near.at[:, 4 * BLOCK : 5 * BLOCK, columns],
            near.at[:, pl.ds(pl.multiple_of(hi * 3 * BLOCK, BLOCK), BLOCK), columns],
            relay_s.at[head], relay_r.at[head], relay_to,
        )
        relays.append(copy)
        if head in WRAP_HEADS:
            pl.when(jnp.logical_not(last))(lambda: copy.start())
            pl.when(last & jnp.logical_not(wraps))(lambda: shift_copy(head).start())
        else:
            copy.start()
        partner_one(1, head)

    l4_copies = []

    def send_four(j, chunk):
        for t in range(2):
            l4[t, x, chunk] = matmul(pool_matrix(16, 64), l3[t, chunk]).astype(BF16)
        part = l4.at[:, x, chunk]
        for d in range(1, NX):
            copy = remote(part, part, l4_s.at[j, d], l4_r.at[j, d], at_x(d))
            copy.start()
            l4_copies.append(copy)

    def ring_step(buf, send, recv, s):
        up, down = (y - (s - 1) + NY) % NY, (y + s - 1) % NY
        if s < 4:
            up, down = buf.at[:, up], buf.at[:, down]
        else:
            up, down = buf.at[0, up], buf.at[1, down]
        copies = [
            remote(up, up, send.at[s - 1, 0], recv.at[s - 1, 0], at_y(1)),
            remote(down, down, send.at[s - 1, 1], recv.at[s - 1, 1], at_y(NY - 1)),
        ]
        for copy in copies:
            copy.start()
        return copies

    ring3 = ring_step(l3, ring3_s, ring3_r, 1)
    send_four(0, y)
    ring2 = ring_step(l2, ring2_s, ring2_r, 1)
    finished = list(ring3) + list(ring2)
    for s in range(1, 5):
        arrive("ring3 %d" % s, *ring3)
        if s < 4:
            ring3 = ring_step(l3, ring3_s, ring3_r, s + 1)
            finished += ring3
            send_four(2 * s - 1, (y - s + NY) % NY)
            send_four(2 * s, (y + s) % NY)
        else:
            send_four(7, (y + 4) % NY)
        arrive("ring2 %d" % s, *ring2)
        if s < 4:
            ring2 = ring_step(l2, ring2_s, ring2_r, s + 1)
            finished += ring2
    def far_keys(buf, columns):
        index = (slice(None),) * (len(buf.shape) - 2) + (columns,)
        return [buf[(t,) + index].reshape(512, HEAD_DIM) for t in range(2)]

    def far(buf):
        def body(head, carry):
            attend(head, 0, 2 * BLOCK, *far_keys(buf, head_columns(head)), None, False)
            return carry

        with scope("far"):
            lax.fori_loop(0, LOCAL_HEADS, body, 0, unroll=True)

    for head in range(LOCAL_HEADS):
        relay(head)
    for copy in near_rest[LATE:]:
        copy.start()

    far(l3)
    far(l2)
    @pl.when(shifted)
    def _():
        for head in WRAP_HEADS:
            shift_copy(head).wait_recv()
            onward_copy(head).start()

    arrive("four along x", *l4_copies)
    far(l4)
    arrive("one along y", l1y)

    out = []

    def finish(head):
        columns = pl.ds(head * HEAD_DIM, HEAD_DIM)
        arrive("relay %d" % head, relays[head])
        key = lax.broadcasted_iota(jnp.int32, (BLOCK, BLOCK), 0)
        query = lax.broadcasted_iota(jnp.int32, (BLOCK, BLOCK), 1)
        for half in range(2):
            edge = slice(half * 3 * BLOCK, half * 3 * BLOCK + BLOCK)
            if half == 0:
                allowed = (key >= query) & (chip > 0)
            else:
                allowed = (key < query) & (chip < CHIPS - 1)
            attend(
                head, half * BLOCK, BLOCK, near[0, edge, columns], near[1, edge, columns],
                allowed, False,
            )
        arrive("one %d" % head, one_parts[head], one_parts[LOCAL_HEADS + head])
        attend(head, 0, 2 * BLOCK, *far_keys(l1, columns), None, False)
        mean = (acc[head] / den[head]).T.astype(BF16)
        for half in range(2):
            result[half, :, columns] = mean[half * BLOCK : (half + 1) * BLOCK]
        place = pl.ds(pl.multiple_of(core * COLS + head * HEAD_DIM, HEAD_DIM), HEAD_DIM)
        away = remote(
            result.at[1 - core, :, columns], o_hbm.at[:, place],
            out_s.at[head], out_r.at[head], sibling,
        )
        away.start()
        here = pltpu.make_async_copy(
            result.at[core, :, columns], o_hbm.at[:, place], out_loc.at[head]
        )
        here.start()
        out.append((away, here))

    for head in range(LOCAL_HEADS + 1):
        if head < LOCAL_HEADS:
            arrive("inner %d" % head, near_copy(0, head, 0), near_copy(0, head, 1))
            partner_one(0, head)
        if head > 0:
            finish(head - 1)
    with scope("sent"):
        for copy in sib + l3z + [l2z, l1y, near_first] + near_rest + finished + l4_copies:
            copy.wait_send()
        for copy in one_parts:
            copy.wait_send()
        for head in range(LOCAL_HEADS):
            if head not in WRAP_HEADS:
                relays[head].wait_send()

        @pl.when(jnp.logical_not(last))
        def _():
            for head in WRAP_HEADS:
                relays[head].wait_send()

        @pl.when(last & jnp.logical_not(wraps))
        def _():
            for head in WRAP_HEADS:
                shift_copy(head).wait_send()

        @pl.when(shifted)
        def _():
            for head in WRAP_HEADS:
                onward_copy(head).wait_send()

        @pl.when(owns_wrap)
        def _():
            for copy in wrap_copies:
                copy.wait_send()

    with scope("result"):
        for away, here in out:
            here.wait()
            away.wait()


def local(query_rows, key_rows, value_rows):
    any_space = pl.BlockSpec(memory_space=pl.ANY)
    dma = pltpu.SemaphoreType.DMA
    return pl.pallas_call(
        kernel,
        out_shape=jax.ShapeDtypeStruct(query_rows.shape, query_rows.dtype),
        in_specs=[pl.BlockSpec(memory_space=pltpu.HBM)] * 3,
        out_specs=any_space,
        scratch_shapes=[
            pltpu.VMEM((2, 6 * BLOCK, COLS), BF16),
            pltpu.VMEM((2 * BLOCK, COLS), BF16),
            pltpu.VMEM((2, 2, N_HI, 128, COLS), BF16),
            pltpu.VMEM((2, NY, N_HI, 32, COLS), BF16),
            pltpu.VMEM((2, NY, 64, COLS), BF16),
            pltpu.VMEM((2, NX, NY, 16, COLS), BF16),
            pltpu.VMEM((NZ, 16, COLS), BF16),
            pltpu.VMEM((LOCAL_HEADS, HEAD_DIM, 2 * BLOCK), F32),
            pltpu.VMEM((LOCAL_HEADS, 1, 2 * BLOCK), F32),
            pltpu.VMEM((LOCAL_HEADS, 1, 2 * BLOCK), F32),
            pltpu.VMEM((2, BLOCK, COLS), BF16),
            dma((3,)), dma((3,)), dma((3,)),
            dma((2, LOCAL_HEADS, 2)), dma((2, LOCAL_HEADS, 2)),
            dma((LOCAL_HEADS,)), dma((LOCAL_HEADS,)), dma((LOCAL_HEADS,)),
            dma((LOCAL_HEADS,)), dma((LOCAL_HEADS,)), dma((LOCAL_HEADS,)), dma((2, LOCAL_HEADS)), dma((2, LOCAL_HEADS)),
            dma((1,)), dma((1,)), dma((NZ,)), dma((NZ,)), dma((3,)), dma((3,)),
            dma((4, 2)), dma((4, 2)), dma((4, 2)), dma((4, 2)),
            dma((NY, NX)), dma((NY, NX)),
            dma((LOCAL_HEADS,)), dma((LOCAL_HEADS,)), dma((LOCAL_HEADS,)),
        ],
        compiler_params=pltpu.CompilerParams(
            collective_id=0, has_side_effects=True, vmem_limit_bytes=53 * 1024 * 1024
        ),
    )(query_rows, key_rows, value_rows)


def solution(mesh):
    spec = P(("seqa", "seqb"), None)
    return jax.shard_map(
        local, mesh=mesh, in_specs=(spec, spec, spec), out_specs=spec, check_vma=False
    )
```

```python
import contextlib

import jax
import jax.numpy as jnp
from jax import lax
from jax.experimental import pallas as pl
from jax.experimental.pallas import tpu as pltpu
from jax.sharding import PartitionSpec as P

MESH = pl.DeviceIdType.MESH
BF16, F32 = jnp.bfloat16, jnp.float32

HEAD_DIM = 128
BLOCK = 256
NX, NY, NZ, NZ_LO, N_HI = 4, 8, 8, 4, 2
CHIPS = 256
LOCAL_HEADS = 4
COLS = LOCAL_HEADS * HEAD_DIM
EXP2_SCALE = 1.4426950408889634 / HEAD_DIM**0.5
MASKED = -1e30
EARLY, LATE = 0, 8
WRAP_HEADS = (3,)


def scope(name):
    return contextlib.nullcontext()


def arrive(name, *copies):
    with scope(name):
        for copy in copies:
            copy.wait_recv()


def pool_matrix(rows, columns):
    row = lax.broadcasted_iota(jnp.int32, (rows, columns), 0)
    column = lax.broadcasted_iota(jnp.int32, (rows, columns), 1)
    return jnp.where((column >> 2) == row, 0.25, 0.0).astype(BF16)


def matmul(a, b):
    return jnp.dot(a, b, preferred_element_type=F32)


def kernel(
    q_hbm, k_hbm, v_hbm, o_hbm,
    near, queries, l1, l2, l3, l4, tile, acc, top, den, result,
    loc_sem, sib_s, sib_r, near_s, near_r, relay_s, relay_r, wrap_s, shift_s, shift_r, onward_s, one_s, one_r, l2z_s, l2z_r, l3z_s, l3z_r, l1_s, l1_r,
    ring2_s, ring2_r, ring3_s, ring3_r, l4_s, l4_r, out_loc, out_s, out_r,
):
    seqa, seqb = lax.axis_index("seqa"), lax.axis_index("seqb")
    x, z_lo = seqa // NZ_LO, seqa % NZ_LO
    y, hi, core = seqb // 4, (seqb // 2) % 2, seqb % 2
    z = hi * NZ_LO + z_lo
    chip = seqa * 16 + seqb // 2

    def at_z(d):
        other = (z + d) % NZ
        return (x * NZ_LO + other % NZ_LO, (y * 2 + other // NZ_LO) * 2 + core)

    def at_y(d):
        return (seqa, (((y + d) % NY) * 2 + hi) * 2 + core)

    def at_x(d):
        return (((x + d) % NX) * NZ_LO + z_lo, seqb)

    sibling = (seqa, seqb + 1 - 2 * core)
    y_pair = (seqa, ((y + 1 - 2 * (y % 2)) * 2 + hi) * 2 + core)
    y_par = y % 2

    last = ((hi == 0) & (y == NY - 1)) | ((hi == 1) & (y == 0))
    first_of_row = ((hi == 0) & (y == 0)) | ((hi == 1) & (y == NY - 1))
    z_partner = at_z(4)
    rows_of_chips = NX * NZ_LO
    relay_to = (
        jnp.where(last, (seqa + rows_of_chips + 1 - 2 * hi) % rows_of_chips, seqa),
        at_y(NY + 1 - 2 * hi)[1],
    )
    relay_from = (
        jnp.where(first_of_row, (seqa + rows_of_chips + 2 * hi - 1) % rows_of_chips, seqa),
        at_y(NY + 2 * hi - 1)[1],
    )

    wraps = jnp.where(hi == 0, z_lo == NZ_LO - 1, z_lo == 0) & last
    owns_wrap = jnp.where(hi == 1, z_lo == NZ_LO - 1, z_lo == 0) & first_of_row
    takes_wrap = jnp.where(hi == 0, z_lo == 0, z_lo == NZ_LO - 1) & first_of_row
    shifted = jnp.where(hi == 0, z_lo > 0, z_lo < NZ_LO - 1) & last
    wrap_to = (
        (seqa + rows_of_chips + 2 * hi - 1) % rows_of_chips,
        (((y + NY + 2 * hi - 1) % NY) * 2 + 1 - hi) * 2 + core,
    )
    wrap_from = wrap_to

    barrier = pltpu.get_barrier_semaphore()
    partners = [sibling, relay_from]
    partners += [at_z(d) for d in range(1, NZ)]
    partners += [at_y(d) for d in (1, 7)] + [at_x(d) for d in (1, 2, 3)]
    with scope("entry"):
        for partner in partners:
            pl.semaphore_signal(barrier, inc=1, device_id=partner, device_id_type=MESH)

        @pl.when(takes_wrap)
        def _():
            pl.semaphore_signal(barrier, inc=1, device_id=wrap_from, device_id_type=MESH)

        pl.semaphore_wait(barrier, len(partners) + jnp.where(owns_wrap, 1, 0))

    def remote(src, dst, s, r, device):
        return pltpu.make_async_remote_copy(
            src_ref=src, dst_ref=dst, send_sem=s, recv_sem=r, device_id=device, device_id_type=MESH
        )

    mine = pl.ds(pl.multiple_of(core * COLS, COLS), COLS)
    theirs = pl.ds(pl.multiple_of((1 - core) * COLS, COLS), COLS)
    own_rows = pl.ds(pl.multiple_of(core * BLOCK, BLOCK), BLOCK)
    sib_rows = pl.ds(pl.multiple_of((1 - core) * BLOCK, BLOCK), BLOCK)
    own_near = pl.ds(pl.multiple_of(BLOCK + core * BLOCK, BLOCK), BLOCK)
    sib_near = pl.ds(pl.multiple_of(2 * BLOCK - core * BLOCK, BLOCK), BLOCK)

    sib = [
        remote(k_hbm.at[:, theirs], near.at[0, own_near], sib_s.at[0], sib_r.at[0], sibling),
        remote(v_hbm.at[:, theirs], near.at[1, own_near], sib_s.at[1], sib_r.at[1], sibling),
        remote(q_hbm.at[:, theirs], queries.at[own_rows], sib_s.at[2], sib_r.at[2], sibling),
    ]
    loc = [
        pltpu.make_async_copy(k_hbm.at[:, mine], near.at[0, own_near], loc_sem.at[0]),
        pltpu.make_async_copy(v_hbm.at[:, mine], near.at[1, own_near], loc_sem.at[1]),
        pltpu.make_async_copy(q_hbm.at[:, mine], queries.at[own_rows], loc_sem.at[2]),
    ]
    for copy in (sib[0], sib[1], loc[0], loc[1], sib[2], loc[2]):
        copy.start()

    own_kind = 1 - (core + hi) % 2

    def near_copy(kind, head, t):
        columns = pl.ds(head * HEAD_DIM, HEAD_DIM)
        block = hi * kind + (1 - hi) * (1 - kind)
        src = near.at[t, pl.ds(pl.multiple_of(BLOCK + block * BLOCK, BLOCK), BLOCK), columns]
        place = 4 * BLOCK * kind + hi * 3 * BLOCK * (1 - kind)
        dst = near.at[t, pl.ds(pl.multiple_of(place, BLOCK), BLOCK), columns]
        return remote(src, dst, near_s.at[kind, head, t], near_r.at[kind, head, t], z_partner)

    loc[0].wait()
    near_first = near_copy(own_kind, 0, 0)
    near_first.start()
    loc[1].wait()
    arrive("sibling rows", sib[0], sib[1])

    tiles = []
    with scope("pooling"):
        for t in range(2):
            one = matmul(pool_matrix(128, 512), near[t, BLOCK : 3 * BLOCK, :]).astype(BF16)
            l1[t, y_par, hi] = one
            two = matmul(pool_matrix(32, 128), one).astype(BF16)
            l2[t, y, hi] = two
            tiles.append(matmul(pool_matrix(16, 32), two)[:8])
        tile[z] = jnp.concatenate(tiles, axis=0).astype(BF16)

    l3z = [
        remote(tile.at[z], tile.at[z], l3z_s.at[d], l3z_r.at[d], at_z(d)) for d in range(1, NZ)
    ]
    for copy in l3z:
        copy.start()
    l2z = remote(l2.at[:, y, hi], l2.at[:, y, hi], l2z_s.at[0], l2z_r.at[0], at_z(4))
    l2z.start()
    own_one = l1.at[:, y_par, hi]
    l1y = remote(own_one, own_one, l1_s.at[1], l1_r.at[1], y_pair)
    l1y.start()
    near_rest = [near_copy(1 - own_kind, 0, 0)] + [
        near_copy(kind, head, t)
        for kind in (1, 0)
        for head in range(LOCAL_HEADS)
        for t in range(2)
        if (head, t) != (0, 0)
    ]
    for copy in near_rest[:EARLY]:
        copy.start()

    def head_columns(head):
        return pl.ds(pl.multiple_of(head * HEAD_DIM, HEAD_DIM), HEAD_DIM)

    def attend(head, first_query, count, keys, values, allowed, first):
        q = queries[first_query : first_query + count, head_columns(head)]
        span = slice(first_query, first_query + count)
        scores = lax.dot_general(keys, q, (((1,), (1,)), ((), ())), preferred_element_type=F32)
        if allowed is not None:
            scores = jnp.where(allowed, scores, MASKED)
        highest = jnp.max(scores, axis=0, keepdims=True)
        if not first:
            old = top[head, :, span]
            highest = jnp.maximum(highest, old)
        weights = jnp.exp2((scores - highest) * EXP2_SCALE)
        total = jnp.sum(weights, axis=0, keepdims=True)
        mixed = lax.dot_general(
            values, weights.astype(BF16), (((0,), (0,)), ((), ())), preferred_element_type=F32
        )
        if not first:
            shrink = jnp.exp2((old - highest) * EXP2_SCALE)
            total = total + den[head, :, span] * shrink
            mixed = mixed + acc[head, :, span] * shrink
        top[head, :, span] = highest
        den[head, :, span] = total
        acc[head, :, span] = mixed

    loc[2].wait()
    sib[2].wait_recv()

    def inner(head, carry):
        columns = head_columns(head)
        key = lax.broadcasted_iota(jnp.int32, (2 * BLOCK, 2 * BLOCK), 0)
        query = lax.broadcasted_iota(jnp.int32, (2 * BLOCK, 2 * BLOCK), 1)
        allowed = (key <= query + BLOCK - 1) & (key >= query - BLOCK)
        keys, values = near[0, BLOCK : 3 * BLOCK, columns], near[1, BLOCK : 3 * BLOCK, columns]
        attend(head, 0, 2 * BLOCK, keys, values, allowed, True)
        return carry

    with scope("inner"):
        lax.fori_loop(0, LOCAL_HEADS, inner, 0, unroll=True)

    arrive("three along z", *l3z)
    arrive("two along z", l2z)
    wrap_copies = [
        remote(
            near.at[:, pl.ds(pl.multiple_of((1 + hi) * BLOCK, BLOCK), BLOCK), columns],
            near.at[:, pl.ds(pl.multiple_of((1 - hi) * 3 * BLOCK, BLOCK), BLOCK), columns],
            wrap_s.at[head], relay_r.at[head], wrap_to,
        )
        for head in WRAP_HEADS
        for columns in [pl.ds(head * HEAD_DIM, HEAD_DIM)]
    ]

    @pl.when(owns_wrap)
    def _():
        for copy in wrap_copies:
            copy.start()

    for copy in near_rest[EARLY:LATE]:
        copy.start()
    for t in range(2):
        rows = [tile[i].astype(F32)[8 * t : 8 * t + 8] for i in range(NZ)]
        l3[t, y] = jnp.concatenate(rows, axis=0).astype(BF16)

    relays, one_parts = [], []

    def partner_one(kind, head):
        columns = pl.ds(head * HEAD_DIM, HEAD_DIM)
        block = (1 - hi) * kind + hi * (1 - kind)
        rows = pl.ds(pl.multiple_of(block * 64, 64), 64)
        place = 4 * BLOCK * kind + (1 - hi) * 3 * BLOCK * (1 - kind)

        for t in range(2):
            block_rows = near[t, pl.ds(pl.multiple_of(place, BLOCK), BLOCK), columns]
            pooled = matmul(pool_matrix(64, BLOCK), block_rows)
            l1[t, y_par, 1 - hi, rows, columns] = pooled.astype(BF16)
        part = l1.at[:, y_par, 1 - hi, rows, columns]
        copy = remote(part, part, one_s.at[kind, head], one_r.at[kind, head], y_pair)
        copy.start()
        one_parts.append(copy)

    def shift_copy(head):
        columns = pl.ds(head * HEAD_DIM, HEAD_DIM)
        return remote(
            near.at[:, 4 * BLOCK : 5 * BLOCK, columns], near.at[:, 5 * BLOCK :, columns],
            shift_s.at[head], shift_r.at[head], at_z(NZ + 1 - 2 * hi),
        )

    def onward_copy(head):
        columns = pl.ds(head * HEAD_DIM, HEAD_DIM)
        return remote(
            near.at[:, 5 * BLOCK :, columns],
            near.at[:, pl.ds(pl.multiple_of(hi * 3 * BLOCK, BLOCK), BLOCK), columns],
            onward_s.at[head], relay_r.at[head], at_y(NY + 1 - 2 * hi),
        )

    def relay(head):
        columns = pl.ds(head * HEAD_DIM, HEAD_DIM)
        arrive("outer %d" % head, near_copy(1, head, 0), near_copy(1, head, 1))
        copy = remote(
            near.at[:, 4 * BLOCK : 5 * BLOCK, columns],
            near.at[:, pl.ds(pl.multiple_of(hi * 3 * BLOCK, BLOCK), BLOCK), columns],
            relay_s.at[head], relay_r.at[head], relay_to,
        )
        relays.append(copy)
        if head in WRAP_HEADS:
            pl.when(jnp.logical_not(last))(lambda: copy.start())
            pl.when(last & jnp.logical_not(wraps))(lambda: shift_copy(head).start())
        else:
            copy.start()
        partner_one(1, head)

    l4_copies = []

    def send_four(j, chunk):
        for t in range(2):
            l4[t, x, chunk] = matmul(pool_matrix(16, 64), l3[t, chunk]).astype(BF16)
        part = l4.at[:, x, chunk]
        for d in range(1, NX):
            copy = remote(part, part, l4_s.at[j, d], l4_r.at[j, d], at_x(d))
            copy.start()
            l4_copies.append(copy)

    def ring_step(buf, send, recv, s):
        up, down = (y - (s - 1) + NY) % NY, (y + s - 1) % NY
        if s < 4:
            up, down = buf.at[:, up], buf.at[:, down]
        else:
            up, down = buf.at[0, up], buf.at[1, down]
        copies = [
            remote(up, up, send.at[s - 1, 0], recv.at[s - 1, 0], at_y(1)),
            remote(down, down, send.at[s - 1, 1], recv.at[s - 1, 1], at_y(NY - 1)),
        ]
        for copy in copies:
            copy.start()
        return copies

    ring3 = ring_step(l3, ring3_s, ring3_r, 1)
    send_four(0, y)
    ring2 = ring_step(l2, ring2_s, ring2_r, 1)
    finished = list(ring3) + list(ring2)
    for s in range(1, 5):
        arrive("ring3 %d" % s, *ring3)
        if s < 4:
            ring3 = ring_step(l3, ring3_s, ring3_r, s + 1)
            finished += ring3
            send_four(2 * s - 1, (y - s + NY) % NY)
            send_four(2 * s, (y + s) % NY)
        else:
            send_four(7, (y + 4) % NY)
        arrive("ring2 %d" % s, *ring2)
        if s < 4:
            ring2 = ring_step(l2, ring2_s, ring2_r, s + 1)
            finished += ring2
    def far_keys(buf, columns):
        index = (slice(None),) * (len(buf.shape) - 2) + (columns,)
        return [buf[(t,) + index].reshape(512, HEAD_DIM) for t in range(2)]

    def far(buf):
        def body(head, carry):
            attend(head, 0, 2 * BLOCK, *far_keys(buf, head_columns(head)), None, False)
            return carry

        with scope("far"):
            lax.fori_loop(0, LOCAL_HEADS, body, 0, unroll=True)

    for head in range(LOCAL_HEADS):
        if head == LOCAL_HEADS - 1:
            near_rest[LATE].start()
        relay(head)
    for copy in near_rest[LATE + 1 :]:
        copy.start()

    far(l3)
    far(l2)
    @pl.when(shifted)
    def _():
        for head in WRAP_HEADS:
            shift_copy(head).wait_recv()
            onward_copy(head).start()

    arrive("four along x", *l4_copies)
    far(l4)
    arrive("one along y", l1y)

    out = []

    def finish(head):
        columns = pl.ds(head * HEAD_DIM, HEAD_DIM)
        arrive("relay %d" % head, relays[head])
        key = lax.broadcasted_iota(jnp.int32, (BLOCK, BLOCK), 0)
        query = lax.broadcasted_iota(jnp.int32, (BLOCK, BLOCK), 1)
        for half in range(2):
            edge = slice(half * 3 * BLOCK, half * 3 * BLOCK + BLOCK)
            if half == 0:
                allowed = (key >= query) & (chip > 0)
            else:
                allowed = (key < query) & (chip < CHIPS - 1)
            attend(
                head, half * BLOCK, BLOCK, near[0, edge, columns], near[1, edge, columns],
                allowed, False,
            )
        arrive("one %d" % head, one_parts[head], one_parts[LOCAL_HEADS + head])
        attend(head, 0, 2 * BLOCK, *far_keys(l1, columns), None, False)
        mean = (acc[head] / den[head]).T.astype(BF16)
        for half in range(2):
            result[half, :, columns] = mean[half * BLOCK : (half + 1) * BLOCK]
        place = pl.ds(pl.multiple_of(core * COLS + head * HEAD_DIM, HEAD_DIM), HEAD_DIM)
        away = remote(
            result.at[1 - core, :, columns], o_hbm.at[:, place],
            out_s.at[head], out_r.at[head], sibling,
        )
        away.start()
        here = pltpu.make_async_copy(
            result.at[core, :, columns], o_hbm.at[:, place], out_loc.at[head]
        )
        here.start()
        out.append((away, here))

    for head in range(LOCAL_HEADS + 1):
        if head < LOCAL_HEADS:
            arrive("inner %d" % head, near_copy(0, head, 0), near_copy(0, head, 1))
            partner_one(0, head)
        if head > 0:
            finish(head - 1)
    with scope("sent"):
        for copy in sib + l3z + [l2z, l1y, near_first] + near_rest + finished + l4_copies:
            copy.wait_send()
        for copy in one_parts:
            copy.wait_send()
        for head in range(LOCAL_HEADS):
            if head not in WRAP_HEADS:
                relays[head].wait_send()

        @pl.when(jnp.logical_not(last))
        def _():
            for head in WRAP_HEADS:
                relays[head].wait_send()

        @pl.when(last & jnp.logical_not(wraps))
        def _():
            for head in WRAP_HEADS:
                shift_copy(head).wait_send()

        @pl.when(shifted)
        def _():
            for head in WRAP_HEADS:
                onward_copy(head).wait_send()

        @pl.when(owns_wrap)
        def _():
            for copy in wrap_copies:
                copy.wait_send()

    with scope("result"):
        for away, here in out:
            here.wait()
            away.wait()


def local(query_rows, key_rows, value_rows):
    any_space = pl.BlockSpec(memory_space=pl.ANY)
    dma = pltpu.SemaphoreType.DMA
    return pl.pallas_call(
        kernel,
        out_shape=jax.ShapeDtypeStruct(query_rows.shape, query_rows.dtype),
        in_specs=[pl.BlockSpec(memory_space=pltpu.HBM)] * 3,
        out_specs=any_space,
        scratch_shapes=[
            pltpu.VMEM((2, 6 * BLOCK, COLS), BF16),
            pltpu.VMEM((2 * BLOCK, COLS), BF16),
            pltpu.VMEM((2, 2, N_HI, 128, COLS), BF16),
            pltpu.VMEM((2, NY, N_HI, 32, COLS), BF16),
            pltpu.VMEM((2, NY, 64, COLS), BF16),
            pltpu.VMEM((2, NX, NY, 16, COLS), BF16),
            pltpu.VMEM((NZ, 16, COLS), BF16),
            pltpu.VMEM((LOCAL_HEADS, HEAD_DIM, 2 * BLOCK), F32),
            pltpu.VMEM((LOCAL_HEADS, 1, 2 * BLOCK), F32),
            pltpu.VMEM((LOCAL_HEADS, 1, 2 * BLOCK), F32),
            pltpu.VMEM((2, BLOCK, COLS), BF16),
            dma((3,)), dma((3,)), dma((3,)),
            dma((2, LOCAL_HEADS, 2)), dma((2, LOCAL_HEADS, 2)),
            dma((LOCAL_HEADS,)), dma((LOCAL_HEADS,)), dma((LOCAL_HEADS,)),
            dma((LOCAL_HEADS,)), dma((LOCAL_HEADS,)), dma((LOCAL_HEADS,)), dma((2, LOCAL_HEADS)), dma((2, LOCAL_HEADS)),
            dma((1,)), dma((1,)), dma((NZ,)), dma((NZ,)), dma((3,)), dma((3,)),
            dma((4, 2)), dma((4, 2)), dma((4, 2)), dma((4, 2)),
            dma((NY, NX)), dma((NY, NX)),
            dma((LOCAL_HEADS,)), dma((LOCAL_HEADS,)), dma((LOCAL_HEADS,)),
        ],
        compiler_params=pltpu.CompilerParams(
            collective_id=0, has_side_effects=True, vmem_limit_bytes=53 * 1024 * 1024
        ),
    )(query_rows, key_rows, value_rows)


def solution(mesh):
    spec = P(("seqa", "seqb"), None)
    return jax.shard_map(
        local, mesh=mesh, in_specs=(spec, spec, spec), out_specs=spec, check_vma=False
    )
```
